32 devices in a mesh: groups: 2 (over x), tm: 16 (over z, y, core).
Axes of the slice: x: 2, y: 2, z: 4, core: 2. Of those that a mesh axis runs over, the one named last changes fastest.
Arguments:
- queries: bfloat16 [16384, 512], P(('groups', 'tm')), parts along dimension 0, may hold values from -6 to 6
- keys: bfloat16 [49152, 512], P(('groups', 'tm')), parts along dimension 0, may hold values from -6 to 6
- values: bfloat16 [49152, 512], P(('groups', 'tm')), parts along dimension 0, may hold values from -6 to 6
- out_grad: bfloat16 [16384, 512], P(('groups', 'tm')), parts along dimension 0, may hold values from -6 to 6
- band_start: int32 [32], P('groups'), parts along dimension 0, may hold values from 0 to 22528, as said below
- band_len: int32 [32], P('groups'), parts along dimension 0, may hold values from 1984 to 2048
Outputs:
- attended: bfloat16 [16384, 512], P(('groups', 'tm')), parts along dimension 0
- query_grad: bfloat16 [16384, 512], P(('groups', 'tm')), parts along dimension 0
- key_grad: bfloat16 [49152, 512], P(('groups', 'tm')), parts along dimension 0
- value_grad: bfloat16 [49152, 512], P(('groups', 'tm')), parts along dimension 0
The draws below stay inside these ranges and needn't reach their ends.
There are 2 independent parts, one for each index of `groups`. The reference program is written for one: setup_inputs(seed, part) draws one part's arguments, and reference() takes and returns one part's arrays. A program takes and returns all parts, laid end to end along the dimension named above; each array names one. Nothing has to cross between parts.
Inputs may be any that keep to these rules, and one draw needn't show every extreme that they name: `band_start`: Nondecreasing; stretch c's band starts at c * 1536 - s with s from 128 to 3 * 512 // 4 (both taken in every draw), clipped to the range below.
All inputs are finite; a program needn't handle non-finite values.
Results may differ from the reference program's by a relative error of at most 0.012.
The reference program's roundings to bfloat16 on the way (of `weights_low` and `score_grad`) count: a program that leaves them out, or rounds other values in their place, can miss the bound.
Values may be sent and summed in bfloat16 or wider, within the bound.
A program may use at most 128 MiB of HBM per device.

```python
import jax
import jax.numpy as jnp
from jax import lax

H = 8
DH = 64
UPC = 512
BAND = 2048
CH_DEV = 1
DM = 512
REACH = 512
FPC = 1536
STRETCHES = 16
UNITS = 8192
FRAMES = 24576


def alignment(key):
    shift_key = jax.random.fold_in(key, 101)
    length_key = jax.random.fold_in(key, 102)
    stretch_ids = jnp.arange(STRETCHES, dtype=jnp.int32)
    shifts = jax.random.randint(shift_key, (STRETCHES,), REACH // 4, 3 * REACH // 4 + 1)
    shifts = jnp.where(stretch_ids == CH_DEV, REACH // 4, shifts)
    shifts = jnp.where(stretch_ids == 3 * CH_DEV - 1, 3 * REACH // 4, shifts)
    starts = jnp.clip(stretch_ids * FPC - shifts, 0, FRAMES - BAND).astype(jnp.int32)
    lengths = jax.random.randint(length_key, (STRETCHES,), BAND - REACH // 8, BAND + 1)
    lengths = jnp.where(stretch_ids == 0, BAND - REACH // 8, lengths)
    lengths = jnp.where((stretch_ids == CH_DEV) | (stretch_ids == 3 * CH_DEV - 1), BAND, lengths)
    return (starts, lengths.astype(jnp.int32))


def draw_band_start(key, part):
    starts, lengths = alignment(key)
    return starts


def draw_band_len(key, part):
    starts, lengths = alignment(key)
    return lengths


def draw_queries(key, part):
    key = jax.random.fold_in(key, 3)
    entries = jnp.clip(jax.random.normal(key, (UNITS, DM), jnp.float32), -6.0, 6.0)
    return entries.astype(jnp.bfloat16)


def draw_keys(key, part):
    key = jax.random.fold_in(key, 4)
    entries = jnp.clip(jax.random.normal(key, (FRAMES, DM), jnp.float32), -6.0, 6.0)
    return entries.astype(jnp.bfloat16)


def block_levels(key, dims, cuts, low, top_value):
    gain = 1.0
    for position, parts in cuts:
        draws = jax.random.uniform(jax.random.fold_in(jax.random.fold_in(key, 6), position), (parts,), jnp.float32, low / len(cuts), top_value / len(cuts))
        gain = gain * jnp.repeat(jnp.exp(draws), dims[position] // parts).reshape((-1,) + (1,) * (len(dims) - 1 - position))
    return gain


def noise(own_key, extent, spread, most, shards=(), kind=jnp.bfloat16):
    values = spread * jax.random.normal(own_key, extent, jnp.float32)
    if shards:
        values = values * block_levels(own_key, extent, shards, -0.22, 0.18)
    return jnp.clip(values, -most, most).astype(kind)


def setup_inputs(seed: int = 0, part: int = 0) -> dict:
    arg_keys = jax.random.split(jax.random.key(seed), 7)
    part_keys = jax.random.split(jax.random.fold_in(arg_keys[6], part), 7)
    return {
        "queries": draw_queries(jax.random.fold_in(jax.random.fold_in(arg_keys[6], part), 71), part),
        "keys": draw_keys(jax.random.fold_in(jax.random.fold_in(arg_keys[6], part), 71), part),
        "values": noise(part_keys[2], (FRAMES, DM), 1.0, 6.0, ((0, 16),)),
        "out_grad": noise(part_keys[3], (UNITS, DM), 1.0, 6.0, ((0, 16),)),
        "band_start": draw_band_start(jax.random.fold_in(jax.random.fold_in(arg_keys[6], part), 71), part),
        "band_len": draw_band_len(jax.random.fold_in(jax.random.fold_in(arg_keys[6], part), 71), part),
    }


SCORE_SCALE = 0.125
MASKED_SCORE = -1.0e30


def band_terms(query_stretch, key_band, value_band, grad_stretch, length):
    query_wide = query_stretch.astype(jnp.float32)
    key_wide = key_band.astype(jnp.float32)
    value_wide = value_band.astype(jnp.float32)
    grad_wide = grad_stretch.astype(jnp.float32)
    scores = jnp.einsum("uhd,bhd->hub", query_wide, key_wide) * SCORE_SCALE
    inside = jnp.arange(BAND, dtype=jnp.int32) < length
    scores = jnp.where(inside[None, None, :], scores, MASKED_SCORE)
    row_max = jnp.max(scores, axis=-1, keepdims=True)
    log_total = row_max + jnp.log(jnp.sum(jnp.exp(scores - row_max), axis=-1, keepdims=True))
    weights = jnp.exp(scores - log_total)
    weights_low = lax.optimization_barrier(weights.astype(jnp.bfloat16)).astype(jnp.float32)
    attended = jnp.einsum("hub,bhd->uhd", weights_low, value_wide).astype(jnp.bfloat16)
    attended_wide = lax.optimization_barrier(attended).astype(jnp.float32)
    row_dot = jnp.einsum("uhd,uhd->hu", grad_wide, attended_wide)
    weight_grad = jnp.einsum("uhd,bhd->hub", grad_wide, value_wide)
    score_grad = (weights * (weight_grad - row_dot[:, :, None]) * SCORE_SCALE).astype(jnp.bfloat16)
    score_wide = lax.optimization_barrier(score_grad).astype(jnp.float32)
    query_grad = jnp.einsum("hub,bhd->uhd", score_wide, key_wide).astype(jnp.bfloat16)
    key_term = jnp.einsum("hub,uhd->bhd", score_wide, query_wide)
    value_term = jnp.einsum("hub,uhd->bhd", weights_low, grad_wide)
    return attended, query_grad, key_term, value_term


def reference(queries, keys, values, out_grad, band_start, band_len):
    query_stretches = queries.reshape(STRETCHES, UPC, H, DH)
    grad_stretches = out_grad.reshape(STRETCHES, UPC, H, DH)
    key_rows = keys.reshape(FRAMES, H, DH)
    value_rows = values.reshape(FRAMES, H, DH)

    def add_stretch(totals, stretch_id):
        key_total, value_total = totals
        band_first = band_start[stretch_id].astype(jnp.int32)
        key_band = lax.dynamic_slice_in_dim(key_rows, band_first, BAND, 0)
        value_band = lax.dynamic_slice_in_dim(value_rows, band_first, BAND, 0)
        attended, query_grad, key_term, value_term = band_terms(
            query_stretches[stretch_id], key_band, value_band, grad_stretches[stretch_id], band_len[stretch_id])
        key_total = lax.dynamic_update_slice_in_dim(
            key_total, lax.dynamic_slice_in_dim(key_total, band_first, BAND, 0) + key_term, band_first, 0)
        value_total = lax.dynamic_update_slice_in_dim(
            value_total, lax.dynamic_slice_in_dim(value_total, band_first, BAND, 0) + value_term, band_first, 0)
        return (key_total, value_total), (attended, query_grad)

    zeros_start = jnp.zeros((FRAMES, H, DH), jnp.float32)
    (key_total, value_total), (attended, query_grad) = lax.scan(
        add_stretch, (zeros_start, zeros_start), jnp.arange(STRETCHES, dtype=jnp.int32))
    return (attended.reshape(UNITS, DM), query_grad.reshape(UNITS, DM),
            key_total.astype(jnp.bfloat16).reshape(FRAMES, DM),
            value_total.astype(jnp.bfloat16).reshape(FRAMES, DM))
```

```python
import functools
import math

import jax
import jax.numpy as jnp
from jax import lax
from jax.experimental import pallas as pl
from jax.experimental.pallas import tpu as pltpu
from jax.sharding import PartitionSpec as P

DH = 64
PAIR = 2 * DH
BAND = 2048
REACH = 512
NEAR = 384
FAR = REACH - NEAR
CHUNK = 256
EXPONENT = 0.125 * math.log2(math.e)
MASKED = -1e30
BF16 = jnp.bfloat16
F32 = jnp.float32


def dot(a, b):
    return jnp.dot(a, b, preferred_element_type=F32)


def kernel(
    n, start_ref, len_ref, q_ref, g_ref, k_hbm, v_hbm,
    att_ref, qg_ref, kg_ref, vg_ref,
    wide, bias, probs, maxima, qtx, qm, gt8, gm, att_t, qg_t, totals,
    out_rim, in_rim,
    local_sem, halo_send, halo_recv, far_send, far_recv,
    rim_send, rim_recv, rfar_send, rfar_recv,
):
    me = lax.axis_index("tm")
    units, width = q_ref.shape
    frames = k_hbm.shape[0]
    pairs = width // PAIR
    span = frames + 2 * REACH
    has_lo = me > 0
    has_hi = me < n - 1
    first = me == 0
    last = me == n - 1
    top = REACH + frames

    def remote(src, dst, send, recv, target):
        return pltpu.make_async_remote_copy(
            src_ref=src, dst_ref=dst, send_sem=send, recv_sem=recv,
            device_id={"tm": target}, device_id_type=pl.DeviceIdType.MESH,
        )

    def halo(t, g, way):
        if way == 0:
            src, dst, target = top - NEAR, REACH - NEAR, me + 1
        else:
            src, dst, target = REACH, top, me - 1
        return remote(
            wide.at[t, g, pl.ds(src, NEAR)], wide.at[t, g, pl.ds(dst, NEAR)],
            halo_send.at[t, g, way], halo_recv.at[t, g, way], target,
        )

    def halo_far(t, g, way):
        if way == 0:
            src, dst, target = top - REACH, 0, me + 1
        else:
            src, dst, target = REACH + NEAR, top + NEAR, me - 1
        return remote(
            wide.at[t, g, pl.ds(src, FAR)], wide.at[t, g, pl.ds(dst, FAR)],
            far_send.at[t, g, way], far_recv.at[t, g, way], target,
        )

    def rim(t, g, way):
        off, target = (0, me + 1) if way == 0 else (FAR, me - 1)
        return remote(
            out_rim.at[t, g, way, pl.ds(off, NEAR)], in_rim.at[t, g, way, pl.ds(off, NEAR)],
            rim_send.at[t, g, way], rim_recv.at[t, g, way], target,
        )

    def rim_far(t, g, way):
        off, target = (NEAR, me + 1) if way == 0 else (0, me - 1)
        return remote(
            out_rim.at[t, g, way, pl.ds(off, FAR)], in_rim.at[t, g, way, pl.ds(off, FAR)],
            rfar_send.at[t, g, way], rfar_recv.at[t, g, way], target,
        )

    def local(t, g):
        src = (k_hbm, v_hbm)[t]
        return pltpu.make_async_copy(
            src.at[:, pl.ds(g * PAIR, PAIR)], wide.at[t, g, pl.ds(REACH, frames)],
            local_sem.at[t, g],
        )

    for g in range(pairs):
        for t in range(2):
            local(t, g).start()

    barrier = pltpu.get_barrier_semaphore()

    @pl.when(has_lo)
    def _():
        pl.semaphore_signal(
            barrier, inc=1, device_id={"tm": me - 1}, device_id_type=pl.DeviceIdType.MESH)

    @pl.when(has_hi)
    def _():
        pl.semaphore_signal(
            barrier, inc=1, device_id={"tm": me + 1}, device_id_type=pl.DeviceIdType.MESH)

    pl.semaphore_wait(barrier, has_lo.astype(jnp.int32) + has_hi.astype(jnp.int32))

    @pl.when(first)
    def _():
        in_rim[:, :, 0] = jnp.zeros((2, pairs, REACH, PAIR), BF16)

    @pl.when((me > 1))
    def _():
        in_rim[:, :, 0, NEAR:] = jnp.zeros((2, pairs, FAR, PAIR), BF16)

    @pl.when(last)
    def _():
        in_rim[:, :, 1] = jnp.zeros((2, pairs, REACH, PAIR), BF16)

    @pl.when((me < n - 2))
    def _():
        in_rim[:, :, 1, :FAR] = jnp.zeros((2, pairs, FAR, PAIR), BF16)

    for g in range(pairs):
        for t in range(2):
            local(t, g).wait()

            @pl.when(has_hi)
            def _():
                halo(t, g, 0).start()

            @pl.when(me == n - 2)
            def _():
                halo_far(t, g, 0).start()

            @pl.when(has_lo)
            def _():
                halo(t, g, 1).start()

            @pl.when(me == 1)
            def _():
                halo_far(t, g, 1).start()

    band_first = start_ref[me] - me * frames + REACH
    band_end = band_first + len_ref[me]
    row_id = lax.broadcasted_iota(jnp.int32, (span, PAIR), 0)
    inside = (row_id >= band_first) & (row_id < band_end)
    bias[...] = jnp.where(inside, 0.0, MASKED).astype(BF16)

    row0 = jnp.where(first, REACH, jnp.where(last, 0, FAR))
    chunks = jnp.where(first | last, BAND, frames + 2 * NEAR) // CHUNK

    def rows_of(i):
        return pl.ds(pl.multiple_of(row0 + i * CHUNK, 128), CHUNK)

    def finish(g):
        for t, out in ((0, kg_ref), (1, vg_ref)):
            @pl.when(has_lo)
            def _():
                rim(t, g, 0).wait_recv()

            @pl.when(me == 1)
            def _():
                rim_far(t, g, 0).wait_recv()

            @pl.when(has_hi)
            def _():
                rim(t, g, 1).wait_recv()

            @pl.when(me == n - 2)
            def _():
                rim_far(t, g, 1).wait_recv()

            cols = pl.ds(pl.multiple_of(g * PAIR, PAIR), PAIR)
            own = totals[t, g, REACH:2 * REACH]
            out[:REACH, cols] = (own + in_rim[t, g, 0].astype(F32)).astype(BF16)
            mid = totals[t, g, 2 * REACH:top - REACH]
            out[REACH:frames - REACH, cols] = mid.astype(BF16)
            own = totals[t, g, top - REACH:top]
            out[frames - REACH:, cols] = (own + in_rim[t, g, 1].astype(F32)).astype(BF16)

    def per_pair(g, _):
        cols = pl.ds(pl.multiple_of(g * PAIR, PAIR), PAIR)
        q = q_ref[:, cols].astype(F32)
        grad = g_ref[:, cols].astype(F32)
        q_t = q.T
        grad_t = grad.T
        feature = lax.broadcasted_iota(jnp.int32, (PAIR, units), 0)
        lane = lax.broadcasted_iota(jnp.int32, (units, PAIR), 1)
        for e in range(2):
            mine_t = (feature < DH) == (e == 0)
            mine = (lane < DH) == (e == 0)
            qtx[e, :PAIR] = jnp.where(mine_t, q_t, 0.0).astype(BF16)
            qtx[e, PAIR:] = jnp.where(feature == 0, 1.0, 0.0).astype(BF16)
            qm[e] = jnp.where(mine, q, 0.0).astype(BF16)
            gt8[e] = jnp.where(mine_t, grad_t * 0.125, 0.0).astype(BF16)
            gm[e] = jnp.where(mine, grad, 0.0).astype(BF16)

        for t in range(2):
            @pl.when(has_lo)
            def _():
                halo(t, g, 0).wait_recv()

            @pl.when(last)
            def _():
                halo_far(t, g, 0).wait_recv()

            @pl.when(has_hi)
            def _():
                halo(t, g, 1).wait_recv()

            @pl.when(first)
            def _():
                halo_far(t, g, 1).wait_recv()

        def scores(i, carry):
            rows = rows_of(i)
            key = jnp.concatenate([wide[0, g, rows], bias[rows]], axis=1)
            new = []
            for e in range(2):
                peak, total = carry[e]
                s = dot(key, qtx[e])
                peak_now = jnp.maximum(peak, jnp.max(s, axis=0, keepdims=True))
                prob = jnp.exp2((s - peak_now) * EXPONENT)
                probs[e, rows] = prob
                maxima[e, i] = peak_now
                total = total * jnp.exp2((peak - peak_now) * EXPONENT)
                new.append((peak_now, total + jnp.sum(prob, axis=0, keepdims=True)))
            return tuple(new)

        none = (jnp.full((1, units), -1e38, F32), jnp.zeros((1, units), F32))
        stats = lax.fori_loop(0, chunks, scores, (none, none))
        inverse = [1.0 / stats[e][1] for e in range(2)]

        def factor(e, i):
            return jnp.exp2((maxima[e, i] - stats[e][0]) * EXPONENT) * inverse[e]

        att_t[...] = jnp.zeros_like(att_t)
        qg_t[...] = jnp.zeros_like(qg_t)

        def attend(i, _):
            rows = rows_of(i)
            value_t = wide[1, g, rows].T
            term = None
            for e in range(2):
                low = (probs[e, rows] * factor(e, i)).astype(BF16)
                half = slice(e * DH, (e + 1) * DH)
                att_t[half] += dot(value_t[half], low)
                part = dot(low, gm[e])
                term = part if term is None else term + part
            totals[1, g, rows] = term
            return 0

        lax.fori_loop(0, chunks, attend, 0)

        attended = att_t[...].astype(BF16).astype(F32)
        att_ref[:, cols] = attended.T.astype(BF16)
        product = attended * grad_t * 0.125
        row_dot = [
            jnp.sum(product[e * DH:(e + 1) * DH], axis=0, keepdims=True) for e in range(2)
        ]

        def backward(i, _):
            rows = rows_of(i)
            value = wide[1, g, rows]
            key_t = wide[0, g, rows].T
            term = None
            for e in range(2):
                weight = probs[e, rows] * factor(e, i)
                score_grad = (weight * (dot(value, gt8[e]) - row_dot[e])).astype(BF16)
                half = slice(e * DH, (e + 1) * DH)
                qg_t[half] += dot(key_t[half], score_grad)
                part = dot(score_grad, qm[e])
                term = part if term is None else term + part
            totals[0, g, rows] = term
            return 0

        lax.fori_loop(0, chunks, backward, 0)
        qg_ref[:, cols] = qg_t[...].T.astype(BF16)

        for t in range(2):
            @pl.when(has_hi)
            def _():
                out_rim[t, g, 0, :NEAR] = totals[t, g, top:top + NEAR].astype(BF16)
                rim(t, g, 0).start()

            @pl.when(first)
            def _():
                out_rim[t, g, 0, NEAR:] = totals[t, g, top + NEAR:].astype(BF16)
                rim_far(t, g, 0).start()

            @pl.when(has_lo)
            def _():
                out_rim[t, g, 1, FAR:] = totals[t, g, FAR:REACH].astype(BF16)
                rim(t, g, 1).start()

            @pl.when(last)
            def _():
                out_rim[t, g, 1, :FAR] = totals[t, g, :FAR].astype(BF16)
                rim_far(t, g, 1).start()

        @pl.when(g > 0)
        def _():
            finish(g - 1)

        return 0

    lax.fori_loop(0, pairs, per_pair, 0)
    finish(pairs - 1)

    for g in range(pairs):
        for t in range(2):
            @pl.when(has_hi)
            def _():
                halo(t, g, 0).wait_send()
                rim(t, g, 0).wait_send()

            @pl.when(has_lo)
            def _():
                halo(t, g, 1).wait_send()
                rim(t, g, 1).wait_send()

            @pl.when(me == n - 2)
            def _():
                halo_far(t, g, 0).wait_send()

            @pl.when(me == 1)
            def _():
                halo_far(t, g, 1).wait_send()

            @pl.when(first)
            def _():
                rim_far(t, g, 0).wait_send()

            @pl.when(last)
            def _():
                rim_far(t, g, 1).wait_send()


def on_device(n, queries, keys, values, out_grad, band_start, band_len):
    units, width = queries.shape
    frames = keys.shape[0]
    pairs = width // PAIR
    span = frames + 2 * REACH
    dma = pltpu.SemaphoreType.DMA
    vmem = pl.BlockSpec(memory_space=pltpu.VMEM)
    smem = pl.BlockSpec(memory_space=pltpu.SMEM)
    anywhere = pl.BlockSpec(memory_space=pl.ANY)
    return pl.pallas_call(
        functools.partial(kernel, n),
        out_shape=(
            jax.ShapeDtypeStruct((units, width), BF16),
            jax.ShapeDtypeStruct((units, width), BF16),
            jax.ShapeDtypeStruct((frames, width), BF16),
            jax.ShapeDtypeStruct((frames, width), BF16),
        ),
        in_specs=[smem, smem, vmem, vmem, anywhere, anywhere],
        out_specs=(vmem, vmem, vmem, vmem),
        scratch_shapes=[
            pltpu.VMEM((2, pairs, span, PAIR), BF16),
            pltpu.VMEM((span, PAIR), BF16),
            pltpu.VMEM((2, span, units), F32),
            pltpu.VMEM((2, span // CHUNK, 1, units), F32),
            pltpu.VMEM((2, 2 * PAIR, units), BF16),
            pltpu.VMEM((2, units, PAIR), BF16),
            pltpu.VMEM((2, PAIR, units), BF16),
            pltpu.VMEM((2, units, PAIR), BF16),
            pltpu.VMEM((PAIR, units), F32),
            pltpu.VMEM((PAIR, units), F32),
            pltpu.VMEM((2, pairs, span, PAIR), F32),
            pltpu.VMEM((2, pairs, 2, REACH, PAIR), BF16),
            pltpu.VMEM((2, pairs, 2, REACH, PAIR), BF16),
            dma((2, pairs)),
        ] + [dma((2, pairs, 2))] * 8,
        compiler_params=pltpu.CompilerParams(
            collective_id=0, has_side_effects=True, vmem_limit_bytes=56 * 2**20
        ),
        name="banded",
    )(band_start, band_len, queries, out_grad, keys, values)


def solution(mesh):
    rows = P(("groups", "tm"), None)
    return jax.shard_map(
        functools.partial(on_device, mesh.shape["tm"]),
        mesh=mesh,
        in_specs=(rows, rows, rows, rows, P("groups"), P("groups")),
        out_specs=(rows, rows, rows, rows),
        check_vma=False,
    )
```

```python
import functools
import math

import jax
import jax.numpy as jnp
from jax import lax
from jax.experimental import pallas as pl
from jax.experimental.pallas import tpu as pltpu
from jax.sharding import PartitionSpec as P

DH = 64
PAIR = 2 * DH
BAND = 2048
REACH = 512
NEAR = 384
FAR = REACH - NEAR
CHUNK = 1152
UNROLL = 1
EXPONENT = 0.125 * math.log2(math.e)
MASKED = -1e30
BF16 = jnp.bfloat16
F32 = jnp.float32


def dot(a, b):
    return jnp.dot(a, b, preferred_element_type=F32)


def kernel(
    n, start_ref, len_ref, q_ref, g_ref, k_hbm, v_hbm,
    att_ref, qg_ref, kg_ref, vg_ref,
    wide, bias, probs, maxima, qtx, qm, gt8, gm, att_t, qg_t, totals,
    out_rim, in_rim,
    local_sem, halo_send, halo_recv, far_send, far_recv,
    rim_send, rim_recv, rfar_send, rfar_recv,
):
    me = lax.axis_index("tm")
    units, width = q_ref.shape
    frames = k_hbm.shape[0]
    pairs = width // PAIR
    span = frames + 2 * REACH
    has_lo = me > 0
    has_hi = me < n - 1
    first = me == 0
    last = me == n - 1
    top = REACH + frames

    def remote(src, dst, send, recv, target):
        return pltpu.make_async_remote_copy(
            src_ref=src, dst_ref=dst, send_sem=send, recv_sem=recv,
            device_id={"tm": target}, device_id_type=pl.DeviceIdType.MESH,
        )

    def halo(t, g, way):
        if way == 0:
            src, dst, target = top - NEAR, REACH - NEAR, me + 1
        else:
            src, dst, target = REACH, top, me - 1
        return remote(
            wide.at[t, g, pl.ds(src, NEAR)], wide.at[t, g, pl.ds(dst, NEAR)],
            halo_send.at[t, g, way], halo_recv.at[t, g, way], target,
        )

    def halo_far(t, g, way):
        if way == 0:
            src, dst, target = top - REACH, 0, me + 1
        else:
            src, dst, target = REACH + NEAR, top + NEAR, me - 1
        return remote(
            wide.at[t, g, pl.ds(src, FAR)], wide.at[t, g, pl.ds(dst, FAR)],
            far_send.at[t, g, way], far_recv.at[t, g, way], target,
        )

    def rim(t, g, way):
        off, target = (0, me + 1) if way == 0 else (FAR, me - 1)
        return remote(
            out_rim.at[t, g, way, pl.ds(off, NEAR)], in_rim.at[t, g, way, pl.ds(off, NEAR)],
            rim_send.at[t, g, way], rim_recv.at[t, g, way], target,
        )

    def rim_far(t, g, way):
        off, target = (NEAR, me + 1) if way == 0 else (0, me - 1)
        return remote(
            out_rim.at[t, g, way, pl.ds(off, FAR)], in_rim.at[t, g, way, pl.ds(off, FAR)],
            rfar_send.at[t, g, way], rfar_recv.at[t, g, way], target,
        )

    def local(t, g):
        src = (k_hbm, v_hbm)[t]
        return pltpu.make_async_copy(
            src.at[:, pl.ds(g * PAIR, PAIR)], wide.at[t, g, pl.ds(REACH, frames)],
            local_sem.at[t, g],
        )

    for g in range(pairs):
        for t in range(2):
            local(t, g).start()

    barrier = pltpu.get_barrier_semaphore()

    @pl.when(has_lo)
    def _():
        pl.semaphore_signal(
            barrier, inc=1, device_id={"tm": me - 1}, device_id_type=pl.DeviceIdType.MESH)

    @pl.when(has_hi)
    def _():
        pl.semaphore_signal(
            barrier, inc=1, device_id={"tm": me + 1}, device_id_type=pl.DeviceIdType.MESH)

    pl.semaphore_wait(barrier, has_lo.astype(jnp.int32) + has_hi.astype(jnp.int32))

    @pl.when(first)
    def _():
        wide[:, :, 2 * FAR:REACH] = jnp.zeros((2, pairs, REACH - 2 * FAR, PAIR), BF16)

    @pl.when(last)
    def _():
        wide[:, :, top:top + 2 * FAR] = jnp.zeros((2, pairs, 2 * FAR, PAIR), BF16)

    @pl.when(first)
    def _():
        in_rim[:, :, 0] = jnp.zeros((2, pairs, REACH, PAIR), BF16)

    @pl.when((me > 1))
    def _():
        in_rim[:, :, 0, NEAR:] = jnp.zeros((2, pairs, FAR, PAIR), BF16)

    @pl.when(last)
    def _():
        in_rim[:, :, 1] = jnp.zeros((2, pairs, REACH, PAIR), BF16)

    @pl.when((me < n - 2))
    def _():
        in_rim[:, :, 1, :FAR] = jnp.zeros((2, pairs, FAR, PAIR), BF16)

    for g in range(pairs):
        for t in range(2):
            local(t, g).wait()

            @pl.when(has_hi)
            def _():
                halo(t, g, 0).start()

            @pl.when(me == n - 2)
            def _():
                halo_far(t, g, 0).start()

            @pl.when(has_lo)
            def _():
                halo(t, g, 1).start()

            @pl.when(me == 1)
            def _():
                halo_far(t, g, 1).start()

    band_first = start_ref[me] - me * frames + REACH
    band_end = band_first + len_ref[me]
    row_id = lax.broadcasted_iota(jnp.int32, (span, PAIR), 0)
    inside = (row_id >= band_first) & (row_id < band_end)
    bias[...] = jnp.where(inside, 0.0, MASKED).astype(BF16)

    row0 = jnp.where(first, 2 * FAR, jnp.where(last, 0, FAR))
    chunks = (frames + 2 * NEAR) // CHUNK

    def rows_of(i):
        return pl.ds(pl.multiple_of(row0 + i * CHUNK, 128), CHUNK)

    def finish(g):
        for t, out in ((0, kg_ref), (1, vg_ref)):
            @pl.when(has_lo)
            def _():
                rim(t, g, 0).wait_recv()

            @pl.when(me == 1)
            def _():
                rim_far(t, g, 0).wait_recv()

            @pl.when(has_hi)
            def _():
                rim(t, g, 1).wait_recv()

            @pl.when(me == n - 2)
            def _():
                rim_far(t, g, 1).wait_recv()

            cols = pl.ds(pl.multiple_of(g * PAIR, PAIR), PAIR)
            own = totals[t, g, REACH:2 * REACH]
            out[:REACH, cols] = (own + in_rim[t, g, 0].astype(F32)).astype(BF16)
            mid = totals[t, g, 2 * REACH:top - REACH]
            out[REACH:frames - REACH, cols] = mid.astype(BF16)
            own = totals[t, g, top - REACH:top]
            out[frames - REACH:, cols] = (own + in_rim[t, g, 1].astype(F32)).astype(BF16)

    def per_pair(g, _):
        cols = pl.ds(pl.multiple_of(g * PAIR, PAIR), PAIR)
        q = q_ref[:, cols].astype(F32)
        grad = g_ref[:, cols].astype(F32)
        q_t = q.T
        grad_t = grad.T
        feature = lax.broadcasted_iota(jnp.int32, (PAIR, units), 0)
        lane = lax.broadcasted_iota(jnp.int32, (units, PAIR), 1)
        for e in range(2):
            mine_t = (feature < DH) == (e == 0)
            mine = (lane < DH) == (e == 0)
            qtx[e, :PAIR] = jnp.where(mine_t, q_t, 0.0).astype(BF16)
            qtx[e, PAIR:] = jnp.where(feature == 0, 1.0, 0.0).astype(BF16)
            qm[e] = jnp.where(mine, q, 0.0).astype(BF16)
            gt8[e] = jnp.where(mine_t, grad_t * 0.125, 0.0).astype(BF16)
            gm[e] = jnp.where(mine, grad, 0.0).astype(BF16)

        for t in range(2):
            @pl.when(has_lo)
            def _():
                halo(t, g, 0).wait_recv()

            @pl.when(last)
            def _():
                halo_far(t, g, 0).wait_recv()

            @pl.when(has_hi)
            def _():
                halo(t, g, 1).wait_recv()

            @pl.when(first)
            def _():
                halo_far(t, g, 1).wait_recv()

        def scores(i, carry):
            rows = rows_of(i)
            key = jnp.concatenate([wide[0, g, rows], bias[rows]], axis=1)
            new = []
            for e in range(2):
                peak, total = carry[e]
                s = dot(key, qtx[e])
                peak_now = jnp.maximum(peak, jnp.max(s, axis=0, keepdims=True))
                prob = jnp.exp2((s - peak_now) * EXPONENT)
                probs[e, rows] = prob
                maxima[e, i] = peak_now
                total = total * jnp.exp2((peak - peak_now) * EXPONENT)
                new.append((peak_now, total + jnp.sum(prob, axis=0, keepdims=True)))
            return tuple(new)

        none = (jnp.full((1, units), -1e38, F32), jnp.zeros((1, units), F32))
        stats = lax.fori_loop(0, chunks, scores, (none, none), unroll=UNROLL)
        inverse = [1.0 / stats[e][1] for e in range(2)]

        def factor(e, i):
            return jnp.exp2((maxima[e, i] - stats[e][0]) * EXPONENT) * inverse[e]

        att_t[...] = jnp.zeros_like(att_t)
        qg_t[...] = jnp.zeros_like(qg_t)

        def attend(i, _):
            rows = rows_of(i)
            value_t = wide[1, g, rows].T
            term = None
            for e in range(2):
                low = (probs[e, rows] * factor(e, i)).astype(BF16)
                half = slice(e * DH, (e + 1) * DH)
                att_t[half] += dot(value_t[half], low)
                part = dot(low, gm[e])
                term = part if term is None else term + part
            totals[1, g, rows] = term
            return 0

        lax.fori_loop(0, chunks, attend, 0, unroll=UNROLL)

        attended = att_t[...].astype(BF16).astype(F32)
        att_ref[:, cols] = attended.T.astype(BF16)
        product = attended * grad_t * 0.125
        row_dot = [
            jnp.sum(product[e * DH:(e + 1) * DH], axis=0, keepdims=True) for e in range(2)
        ]

        def backward(i, _):
            rows = rows_of(i)
            value = wide[1, g, rows]
            key_t = wide[0, g, rows].T
            term = None
            for e in range(2):
                weight = probs[e, rows] * factor(e, i)
                score_grad = (weight * (dot(value, gt8[e]) - row_dot[e])).astype(BF16)
                half = slice(e * DH, (e + 1) * DH)
                qg_t[half] += dot(key_t[half], score_grad)
                part = dot(score_grad, qm[e])
                term = part if term is None else term + part
            totals[0, g, rows] = term
            return 0

        lax.fori_loop(0, chunks, backward, 0, unroll=UNROLL)
        qg_ref[:, cols] = qg_t[...].T.astype(BF16)

        for t in range(2):
            @pl.when(has_hi)
            def _():
                out_rim[t, g, 0, :NEAR] = totals[t, g, top:top + NEAR].astype(BF16)
                rim(t, g, 0).start()

            @pl.when(first)
            def _():
                out_rim[t, g, 0, NEAR:] = totals[t, g, top + NEAR:].astype(BF16)
                rim_far(t, g, 0).start()

            @pl.when(has_lo)
            def _():
                out_rim[t, g, 1, FAR:] = totals[t, g, FAR:REACH].astype(BF16)
                rim(t, g, 1).start()

            @pl.when(last)
            def _():
                out_rim[t, g, 1, :FAR] = totals[t, g, :FAR].astype(BF16)
                rim_far(t, g, 1).start()

        @pl.when(g > 0)
        def _():
            finish(g - 1)

        return 0

    lax.fori_loop(0, pairs, per_pair, 0)
    finish(pairs - 1)

    for g in range(pairs):
        for t in range(2):
            @pl.when(has_hi)
            def _():
                halo(t, g, 0).wait_send()
                rim(t, g, 0).wait_send()

            @pl.when(has_lo)
            def _():
                halo(t, g, 1).wait_send()
                rim(t, g, 1).wait_send()

            @pl.when(me == n - 2)
            def _():
                halo_far(t, g, 0).wait_send()

            @pl.when(me == 1)
            def _():
                halo_far(t, g, 1).wait_send()

            @pl.when(first)
            def _():
                rim_far(t, g, 0).wait_send()

            @pl.when(last)
            def _():
                rim_far(t, g, 1).wait_send()


def on_device(n, queries, keys, values, out_grad, band_start, band_len):
    units, width = queries.shape
    frames = keys.shape[0]
    pairs = width // PAIR
    span = frames + 2 * REACH
    dma = pltpu.SemaphoreType.DMA
    vmem = pl.BlockSpec(memory_space=pltpu.VMEM)
    smem = pl.BlockSpec(memory_space=pltpu.SMEM)
    anywhere = pl.BlockSpec(memory_space=pl.ANY)
    return pl.pallas_call(
        functools.partial(kernel, n),
        out_shape=(
            jax.ShapeDtypeStruct((units, width), BF16),
            jax.ShapeDtypeStruct((units, width), BF16),
            jax.ShapeDtypeStruct((frames, width), BF16),
            jax.ShapeDtypeStruct((frames, width), BF16),
        ),
        in_specs=[smem, smem, vmem, vmem, anywhere, anywhere],
        out_specs=(vmem, vmem, vmem, vmem),
        scratch_shapes=[
            pltpu.VMEM((2, pairs, span, PAIR), BF16),
            pltpu.VMEM((span, PAIR), BF16),
            pltpu.VMEM((2, span, units), F32),
            pltpu.VMEM((2, span // CHUNK + 1, 1, units), F32),
            pltpu.VMEM((2, 2 * PAIR, units), BF16),
            pltpu.VMEM((2, units, PAIR), BF16),
            pltpu.VMEM((2, PAIR, units), BF16),
            pltpu.VMEM((2, units, PAIR), BF16),
            pltpu.VMEM((PAIR, units), F32),
            pltpu.VMEM((PAIR, units), F32),
            pltpu.VMEM((2, pairs, span, PAIR), F32),
            pltpu.VMEM((2, pairs, 2, REACH, PAIR), BF16),
            pltpu.VMEM((2, pairs, 2, REACH, PAIR), BF16),
            dma((2, pairs)),
        ] + [dma((2, pairs, 2))] * 8,
        compiler_params=pltpu.CompilerParams(
            collective_id=0, has_side_effects=True, vmem_limit_bytes=56 * 2**20
        ),
        name="banded",
    )(band_start, band_len, queries, out_grad, keys, values)


def solution(mesh):
    rows = P(("groups", "tm"), None)
    return jax.shard_map(
        functools.partial(on_device, mesh.shape["tm"]),
        mesh=mesh,
        in_specs=(rows, rows, rows, rows, P("groups"), P("groups")),
        out_specs=(rows, rows, rows, rows),
        check_vma=False,
    )
```

```python
import functools
import math

import jax
import jax.numpy as jnp
from jax import lax
from jax.experimental import pallas as pl
from jax.experimental.pallas import tpu as pltpu
from jax.sharding import PartitionSpec as P

DH = 64
PAIR = 2 * DH
BAND = 2048
REACH = 512
NEAR = 384
FAR = REACH - NEAR
CHUNK = 1152
UNROLL = 1
PARTS = 4
EXPONENT = 0.125 * math.log2(math.e)
MASKED = -1e30
BF16 = jnp.bfloat16
F32 = jnp.float32


def dot(a, b):
    return jnp.dot(a, b, preferred_element_type=F32)


def kernel(
    n, start_ref, len_ref, q_ref, g_ref, k_hbm, v_hbm,
    att_ref, qg_ref, kg_ref, vg_ref,
    wide, bias, probs, maxima, qtx, qm, gt8, gm, att_t, qg_t, totals,
    out_rim, in_rim,
    local_sem, halo_send, halo_recv, far_send, far_recv,
    rim_send, rim_recv, rfar_send, rfar_recv,
):
    me = lax.axis_index("tm")
    units, width = q_ref.shape
    frames = k_hbm.shape[0]
    pairs = width // PAIR
    span = frames + 2 * REACH
    has_lo = me > 0
    has_hi = me < n - 1
    first = me == 0
    last = me == n - 1
    top = REACH + frames

    def remote(src, dst, send, recv, target):
        return pltpu.make_async_remote_copy(
            src_ref=src, dst_ref=dst, send_sem=send, recv_sem=recv,
            device_id={"tm": target}, device_id_type=pl.DeviceIdType.MESH,
        )

    def halo(t, g, way):
        if way == 0:
            src, dst, target = top - NEAR, REACH - NEAR, me + 1
        else:
            src, dst, target = REACH, top, me - 1
        return remote(
            wide.at[t, g, pl.ds(src, NEAR)], wide.at[t, g, pl.ds(dst, NEAR)],
            halo_send.at[t, g, way], halo_recv.at[t, g, way], target,
        )

    def halo_far(t, g, way):
        if way == 0:
            src, dst, target = top - REACH, 0, me + 1
        else:
            src, dst, target = REACH + NEAR, top + NEAR, me - 1
        return remote(
            wide.at[t, g, pl.ds(src, FAR)], wide.at[t, g, pl.ds(dst, FAR)],
            far_send.at[t, g, way], far_recv.at[t, g, way], target,
        )

    def rim(t, g, way):
        off, target = (0, me + 1) if way == 0 else (FAR, me - 1)
        return remote(
            out_rim.at[t, g, way, pl.ds(off, NEAR)], in_rim.at[t, g, way, pl.ds(off, NEAR)],
            rim_send.at[t, g, way], rim_recv.at[t, g, way], target,
        )

    def rim_far(t, g, way):
        off, target = (NEAR, me + 1) if way == 0 else (0, me - 1)
        return remote(
            out_rim.at[t, g, way, pl.ds(off, FAR)], in_rim.at[t, g, way, pl.ds(off, FAR)],
            rfar_send.at[t, g, way], rfar_recv.at[t, g, way], target,
        )

    def local(t, g):
        src = (k_hbm, v_hbm)[t]
        return pltpu.make_async_copy(
            src.at[:, pl.ds(g * PAIR, PAIR)], wide.at[t, g, pl.ds(REACH, frames)],
            local_sem.at[t, g],
        )

    for g in range(pairs):
        for t in range(2):
            local(t, g).start()

    barrier = pltpu.get_barrier_semaphore()

    @pl.when(has_lo)
    def _():
        pl.semaphore_signal(
            barrier, inc=1, device_id={"tm": me - 1}, device_id_type=pl.DeviceIdType.MESH)

    @pl.when(has_hi)
    def _():
        pl.semaphore_signal(
            barrier, inc=1, device_id={"tm": me + 1}, device_id_type=pl.DeviceIdType.MESH)

    pl.semaphore_wait(barrier, has_lo.astype(jnp.int32) + has_hi.astype(jnp.int32))

    @pl.when(first)
    def _():
        wide[:, :, 2 * FAR:REACH] = jnp.zeros((2, pairs, REACH - 2 * FAR, PAIR), BF16)

    @pl.when(last)
    def _():
        wide[:, :, top:top + 2 * FAR] = jnp.zeros((2, pairs, 2 * FAR, PAIR), BF16)

    @pl.when(first)
    def _():
        in_rim[:, :, 0] = jnp.zeros((2, pairs, REACH, PAIR), BF16)

    @pl.when((me > 1))
    def _():
        in_rim[:, :, 0, NEAR:] = jnp.zeros((2, pairs, FAR, PAIR), BF16)

    @pl.when(last)
    def _():
        in_rim[:, :, 1] = jnp.zeros((2, pairs, REACH, PAIR), BF16)

    @pl.when((me < n - 2))
    def _():
        in_rim[:, :, 1, :FAR] = jnp.zeros((2, pairs, FAR, PAIR), BF16)

    for g in range(pairs):
        for t in range(2):
            local(t, g).wait()

            @pl.when(has_hi)
            def _():
                halo(t, g, 0).start()

            @pl.when(me == n - 2)
            def _():
                halo_far(t, g, 0).start()

            @pl.when(has_lo)
            def _():
                halo(t, g, 1).start()

            @pl.when(me == 1)
            def _():
                halo_far(t, g, 1).start()

    band_first = start_ref[me] - me * frames + REACH
    band_end = band_first + len_ref[me]
    row_id = lax.broadcasted_iota(jnp.int32, (span, PAIR), 0)
    inside = (row_id >= band_first) & (row_id < band_end)
    bias[...] = jnp.where(inside, 0.0, MASKED).astype(BF16)

    row0 = jnp.where(first, 2 * FAR, jnp.where(last, 0, FAR))
    chunks = (frames + 2 * NEAR) // CHUNK

    def rows_of(i):
        return pl.ds(pl.multiple_of(row0 + i * CHUNK, 128), CHUNK)

    def finish(g):
        cols = pl.ds(pl.multiple_of(g * PAIR, PAIR), PAIR)
        for t, out in ((1, vg_ref), (0, kg_ref)):
            mid = totals[t, g, 2 * REACH:top - REACH]
            out[REACH:frames - REACH, cols] = mid.astype(BF16)

        for t, out in ((1, vg_ref), (0, kg_ref)):
            @pl.when(has_lo)
            def _():
                rim(t, g, 0).wait_recv()

            @pl.when(me == 1)
            def _():
                rim_far(t, g, 0).wait_recv()

            @pl.when(has_hi)
            def _():
                rim(t, g, 1).wait_recv()

            @pl.when(me == n - 2)
            def _():
                rim_far(t, g, 1).wait_recv()

            own = totals[t, g, REACH:2 * REACH]
            out[:REACH, cols] = (own + in_rim[t, g, 0].astype(F32)).astype(BF16)
            own = totals[t, g, top - REACH:top]
            out[frames - REACH:, cols] = (own + in_rim[t, g, 1].astype(F32)).astype(BF16)

    def arrived(t, g):
        @pl.when(has_lo)
        def _():
            halo(t, g, 0).wait_recv()

        @pl.when(last)
        def _():
            halo_far(t, g, 0).wait_recv()

        @pl.when(has_hi)
        def _():
            halo(t, g, 1).wait_recv()

        @pl.when(first)
        def _():
            halo_far(t, g, 1).wait_recv()

    def send_rims(t, g):
        @pl.when(has_hi)
        def _():
            out_rim[t, g, 0, :NEAR] = totals[t, g, top:top + NEAR].astype(BF16)
            rim(t, g, 0).start()

        @pl.when(first)
        def _():
            out_rim[t, g, 0, NEAR:] = totals[t, g, top + NEAR:].astype(BF16)
            rim_far(t, g, 0).start()

        @pl.when(has_lo)
        def _():
            out_rim[t, g, 1, FAR:] = totals[t, g, FAR:REACH].astype(BF16)
            rim(t, g, 1).start()

        @pl.when(last)
        def _():
            out_rim[t, g, 1, :FAR] = totals[t, g, :FAR].astype(BF16)
            rim_far(t, g, 1).start()

    def per_pair(g, _):
        cols = pl.ds(pl.multiple_of(g * PAIR, PAIR), PAIR)
        q = q_ref[:, cols].astype(F32)
        grad = g_ref[:, cols].astype(F32)
        q_t = q.T
        grad_t = grad.T
        feature = lax.broadcasted_iota(jnp.int32, (PAIR, units), 0)
        lane = lax.broadcasted_iota(jnp.int32, (units, PAIR), 1)
        for e in range(2):
            mine_t = (feature < DH) == (e == 0)
            mine = (lane < DH) == (e == 0)
            qtx[e, :PAIR] = jnp.where(mine_t, q_t, 0.0).astype(BF16)
            qtx[e, PAIR:] = jnp.where(feature == 0, 1.0, 0.0).astype(BF16)
            qm[e] = jnp.where(mine, q, 0.0).astype(BF16)
            gt8[e] = jnp.where(mine_t, grad_t * 0.125, 0.0).astype(BF16)
            gm[e] = jnp.where(mine, grad, 0.0).astype(BF16)

        arrived(0, g)

        def scores(i, carry):
            rows = rows_of(i)
            key = jnp.concatenate([wide[0, g, rows], bias[rows]], axis=1)
            new = []
            for e in range(2):
                peak, total = carry[e]
                s = dot(key, qtx[e])
                peak_now = jnp.maximum(peak, jnp.max(s, axis=0, keepdims=True))
                prob = jnp.exp2((s - peak_now) * EXPONENT)
                probs[e, rows] = prob
                maxima[e, i] = peak_now
                total = total * jnp.exp2((peak - peak_now) * EXPONENT)
                new.append((peak_now, total + jnp.sum(prob, axis=0, keepdims=True)))
            return tuple(new)

        none = (jnp.full((1, units), -1e38, F32), jnp.zeros((1, units), F32))
        stats = lax.fori_loop(0, chunks, scores, (none, none), unroll=UNROLL)
        inverse = [1.0 / stats[e][1] for e in range(2)]

        def factor(e, i):
            return jnp.exp2((maxima[e, i] - stats[e][0]) * EXPONENT) * inverse[e]

        att_t[...] = jnp.zeros_like(att_t)
        qg_t[...] = jnp.zeros_like(qg_t)

        def attend(i, _):
            rows = rows_of(i)
            value_t = wide[1, g, rows].T
            term = None
            for e in range(2):
                low = (probs[e, rows] * factor(e, i)).astype(BF16)
                half = slice(e * DH, (e + 1) * DH)
                att_t[half] += dot(value_t[half], low)
                part = dot(low, gm[e])
                term = part if term is None else term + part
            totals[1, g, rows] = term
            return 0

        arrived(1, g)
        lax.fori_loop(0, chunks, attend, 0, unroll=UNROLL)
        send_rims(1, g)

        attended = att_t[...].astype(BF16).astype(F32)
        att_ref[:, cols] = attended.T.astype(BF16)
        product = attended * grad_t * 0.125
        row_dot = [
            jnp.sum(product[e * DH:(e + 1) * DH], axis=0, keepdims=True) for e in range(2)
        ]

        def backward(i, _):
            rows = rows_of(i)
            value = wide[1, g, rows]
            key_t = wide[0, g, rows].T
            term = None
            for e in range(2):
                weight = probs[e, rows] * factor(e, i)
                score_grad = (weight * (dot(value, gt8[e]) - row_dot[e])).astype(BF16)
                half = slice(e * DH, (e + 1) * DH)
                qg_t[half] += dot(key_t[half], score_grad)
                part = dot(score_grad, qm[e])
                term = part if term is None else term + part
            totals[0, g, rows] = term
            return 0

        lax.fori_loop(0, chunks, backward, 0, unroll=UNROLL)
        send_rims(0, g)
        qg_ref[:, cols] = qg_t[...].T.astype(BF16)

        @pl.when(g > 0)
        def _():
            finish(g - 1)

        return 0

    lax.fori_loop(0, pairs, per_pair, 0)
    finish(pairs - 1)

    for g in range(pairs):
        for t in range(2):
            @pl.when(has_hi)
            def _():
                halo(t, g, 0).wait_send()
                rim(t, g, 0).wait_send()

            @pl.when(has_lo)
            def _():
                halo(t, g, 1).wait_send()
                rim(t, g, 1).wait_send()

            @pl.when(me == n - 2)
            def _():
                halo_far(t, g, 0).wait_send()

            @pl.when(me == 1)
            def _():
                halo_far(t, g, 1).wait_send()

            @pl.when(first)
            def _():
                rim_far(t, g, 0).wait_send()

            @pl.when(last)
            def _():
                rim_far(t, g, 1).wait_send()


def hand_on(*refs):
    srcs, dsts, sem = refs[:4], refs[4:8], refs[8]
    copies = []
    for a in range(4):
        part = srcs[a].shape[0] // PARTS
        for b in range(PARTS):
            rows = pl.ds(b * part, part)
            copies.append(pltpu.make_async_copy(srcs[a].at[rows], dsts[a].at[rows], sem.at[a, b]))
    for copy in copies:
        copy.start()
    for copy in copies:
        copy.wait()


def on_device(n, queries, keys, values, out_grad, band_start, band_len):
    units, width = queries.shape
    frames = keys.shape[0]
    pairs = width // PAIR
    span = frames + 2 * REACH
    dma = pltpu.SemaphoreType.DMA
    vmem = pl.BlockSpec(memory_space=pltpu.VMEM)
    smem = pl.BlockSpec(memory_space=pltpu.SMEM)
    anywhere = pl.BlockSpec(memory_space=pl.ANY)
    results = pl.pallas_call(
        functools.partial(kernel, n),
        out_shape=(
            jax.ShapeDtypeStruct((units, width), BF16),
            jax.ShapeDtypeStruct((units, width), BF16),
            jax.ShapeDtypeStruct((frames, width), BF16),
            jax.ShapeDtypeStruct((frames, width), BF16),
        ),
        in_specs=[smem, smem, vmem, vmem, anywhere, anywhere],
        out_specs=(vmem, vmem, vmem, vmem),
        scratch_shapes=[
            pltpu.VMEM((2, pairs, span, PAIR), BF16),
            pltpu.VMEM((span, PAIR), BF16),
            pltpu.VMEM((2, span, units), F32),
            pltpu.VMEM((2, span // CHUNK + 1, 1, units), F32),
            pltpu.VMEM((2, 2 * PAIR, units), BF16),
            pltpu.VMEM((2, units, PAIR), BF16),
            pltpu.VMEM((2, PAIR, units), BF16),
            pltpu.VMEM((2, units, PAIR), BF16),
            pltpu.VMEM((PAIR, units), F32),
            pltpu.VMEM((PAIR, units), F32),
            pltpu.VMEM((2, pairs, span, PAIR), F32),
            pltpu.VMEM((2, pairs, 2, REACH, PAIR), BF16),
            pltpu.VMEM((2, pairs, 2, REACH, PAIR), BF16),
            dma((2, pairs)),
        ] + [dma((2, pairs, 2))] * 8,
        compiler_params=pltpu.CompilerParams(
            collective_id=0, has_side_effects=True, vmem_limit_bytes=56 * 2**20
        ),
        name="banded",
    )(band_start, band_len, queries, out_grad, keys, values)
    return pl.pallas_call(
        hand_on,
        out_shape=tuple(jax.ShapeDtypeStruct(r.shape, r.dtype) for r in results),
        in_specs=[vmem] * 4,
        out_specs=(anywhere,) * 4,
        scratch_shapes=[dma((4, PARTS))],
        name="hand_on",
    )(*results)


def solution(mesh):
    rows = P(("groups", "tm"), None)
    return jax.shard_map(
        functools.partial(on_device, mesh.shape["tm"]),
        mesh=mesh,
        in_specs=(rows, rows, rows, rows, P("groups"), P("groups")),
        out_specs=(rows, rows, rows, rows),
        check_vma=False,
    )
```

```python
import functools
import math

import jax
import jax.numpy as jnp
from jax import lax
from jax.experimental import pallas as pl
from jax.experimental.pallas import tpu as pltpu
from jax.sharding import PartitionSpec as P

DH = 64
PAIR = 2 * DH
BAND = 2048
REACH = 512
NEAR = 384
FAR = REACH - NEAR
CHUNK = 384
UNROLL = 6
PARTS = 4
EXPONENT = 0.125 * math.log2(math.e)
MASKED = -1e30
BF16 = jnp.bfloat16
F32 = jnp.float32


def dot(a, b):
    return jnp.dot(a, b, preferred_element_type=F32)


def kernel(
    n, start_ref, len_ref, q_ref, g_ref, k_hbm, v_hbm,
    att_ref, qg_ref, kg_ref, vg_ref,
    wide, bias, probs, maxima, qtx, qm, gt8, gm, att_t, qg_t, totals,
    out_rim, in_rim,
    local_sem, halo_send, halo_recv, far_send, far_recv,
    rim_send, rim_recv, rfar_send, rfar_recv,
):
    me = lax.axis_index("tm")
    units, width = q_ref.shape
    frames = k_hbm.shape[0]
    pairs = width // PAIR
    span = frames + 2 * REACH
    has_lo = me > 0
    has_hi = me < n - 1
    first = me == 0
    last = me == n - 1
    top = REACH + frames

    def remote(src, dst, send, recv, target):
        return pltpu.make_async_remote_copy(
            src_ref=src, dst_ref=dst, send_sem=send, recv_sem=recv,
            device_id={"tm": target}, device_id_type=pl.DeviceIdType.MESH,
        )

    def halo(t, g, way):
        if way == 0:
            src, dst, target = top - NEAR, REACH - NEAR, me + 1
        else:
            src, dst, target = REACH, top, me - 1
        return remote(
            wide.at[t, g, pl.ds(src, NEAR)], wide.at[t, g, pl.ds(dst, NEAR)],
            halo_send.at[t, g, way], halo_recv.at[t, g, way], target,
        )

    def halo_far(t, g, way):
        if way == 0:
            src, dst, target = top - REACH, 0, me + 1
        else:
            src, dst, target = REACH + NEAR, top + NEAR, me - 1
        return remote(
            wide.at[t, g, pl.ds(src, FAR)], wide.at[t, g, pl.ds(dst, FAR)],
            far_send.at[t, g, way], far_recv.at[t, g, way], target,
        )

    def rim(t, g, way):
        off, target = (0, me + 1) if way == 0 else (FAR, me - 1)
        return remote(
            out_rim.at[t, g, way, pl.ds(off, NEAR)], in_rim.at[t, g, way, pl.ds(off, NEAR)],
            rim_send.at[t, g, way], rim_recv.at[t, g, way], target,
        )

    def rim_far(t, g, way):
        off, target = (NEAR, me + 1) if way == 0 else (0, me - 1)
        return remote(
            out_rim.at[t, g, way, pl.ds(off, FAR)], in_rim.at[t, g, way, pl.ds(off, FAR)],
            rfar_send.at[t, g, way], rfar_recv.at[t, g, way], target,
        )

    def local(t, g):
        src = (k_hbm, v_hbm)[t]
        return pltpu.make_async_copy(
            src.at[:, pl.ds(g * PAIR, PAIR)], wide.at[t, g, pl.ds(REACH, frames)],
            local_sem.at[t, g],
        )

    for g in range(pairs):
        for t in range(2):
            local(t, g).start()

    barrier = pltpu.get_barrier_semaphore()

    @pl.when(has_lo)
    def _():
        pl.semaphore_signal(
            barrier, inc=1, device_id={"tm": me - 1}, device_id_type=pl.DeviceIdType.MESH)

    @pl.when(has_hi)
    def _():
        pl.semaphore_signal(
            barrier, inc=1, device_id={"tm": me + 1}, device_id_type=pl.DeviceIdType.MESH)

    pl.semaphore_wait(barrier, has_lo.astype(jnp.int32) + has_hi.astype(jnp.int32))

    @pl.when(first)
    def _():
        wide[:, :, 2 * FAR:REACH] = jnp.zeros((2, pairs, REACH - 2 * FAR, PAIR), BF16)

    @pl.when(last)
    def _():
        wide[:, :, top:top + 2 * FAR] = jnp.zeros((2, pairs, 2 * FAR, PAIR), BF16)

    @pl.when(first)
    def _():
        in_rim[:, :, 0] = jnp.zeros((2, pairs, REACH, PAIR), BF16)

    @pl.when((me > 1))
    def _():
        in_rim[:, :, 0, NEAR:] = jnp.zeros((2, pairs, FAR, PAIR), BF16)

    @pl.when(last)
    def _():
        in_rim[:, :, 1] = jnp.zeros((2, pairs, REACH, PAIR), BF16)

    @pl.when((me < n - 2))
    def _():
        in_rim[:, :, 1, :FAR] = jnp.zeros((2, pairs, FAR, PAIR), BF16)

    for g in range(pairs):
        for t in range(2):
            local(t, g).wait()

            @pl.when(has_hi)
            def _():
                halo(t, g, 0).start()

            @pl.when(me == n - 2)
            def _():
                halo_far(t, g, 0).start()

            @pl.when(has_lo)
            def _():
                halo(t, g, 1).start()

            @pl.when(me == 1)
            def _():
                halo_far(t, g, 1).start()

    band_first = start_ref[me] - me * frames + REACH
    band_end = band_first + len_ref[me]
    row_id = lax.broadcasted_iota(jnp.int32, (span, PAIR), 0)
    inside = (row_id >= band_first) & (row_id < band_end)
    bias[...] = jnp.where(inside, 0.0, MASKED).astype(BF16)

    row0 = jnp.where(first, 2 * FAR, jnp.where(last, 0, FAR))
    chunks = (frames + 2 * NEAR) // CHUNK

    def rows_of(i):
        return pl.ds(pl.multiple_of(row0 + i * CHUNK, 128), CHUNK)

    def finish(g):
        cols = pl.ds(pl.multiple_of(g * PAIR, PAIR), PAIR)
        for t, out in ((1, vg_ref), (0, kg_ref)):
            mid = totals[t, g, 2 * REACH:top - REACH]
            out[REACH:frames - REACH, cols] = mid.astype(BF16)

        for t, out in ((1, vg_ref), (0, kg_ref)):
            @pl.when(has_lo)
            def _():
                rim(t, g, 0).wait_recv()

            @pl.when(me == 1)
            def _():
                rim_far(t, g, 0).wait_recv()

            @pl.when(has_hi)
            def _():
                rim(t, g, 1).wait_recv()

            @pl.when(me == n - 2)
            def _():
                rim_far(t, g, 1).wait_recv()

            own = totals[t, g, REACH:2 * REACH]
            out[:REACH, cols] = (own + in_rim[t, g, 0].astype(F32)).astype(BF16)
            own = totals[t, g, top - REACH:top]
            out[frames - REACH:, cols] = (own + in_rim[t, g, 1].astype(F32)).astype(BF16)

    def arrived(t, g):
        @pl.when(has_lo)
        def _():
            halo(t, g, 0).wait_recv()

        @pl.when(last)
        def _():
            halo_far(t, g, 0).wait_recv()

        @pl.when(has_hi)
        def _():
            halo(t, g, 1).wait_recv()

        @pl.when(first)
        def _():
            halo_far(t, g, 1).wait_recv()

    def send_rims(t, g):
        @pl.when(has_hi)
        def _():
            out_rim[t, g, 0, :NEAR] = totals[t, g, top:top + NEAR].astype(BF16)
            rim(t, g, 0).start()

        @pl.when(first)
        def _():
            out_rim[t, g, 0, NEAR:] = totals[t, g, top + NEAR:].astype(BF16)
            rim_far(t, g, 0).start()

        @pl.when(has_lo)
        def _():
            out_rim[t, g, 1, FAR:] = totals[t, g, FAR:REACH].astype(BF16)
            rim(t, g, 1).start()

        @pl.when(last)
        def _():
            out_rim[t, g, 1, :FAR] = totals[t, g, :FAR].astype(BF16)
            rim_far(t, g, 1).start()

    def per_pair(g, _):
        cols = pl.ds(pl.multiple_of(g * PAIR, PAIR), PAIR)
        q = q_ref[:, cols].astype(F32)
        grad = g_ref[:, cols].astype(F32)
        q_t = q.T
        grad_t = grad.T
        feature = lax.broadcasted_iota(jnp.int32, (PAIR, units), 0)
        lane = lax.broadcasted_iota(jnp.int32, (units, PAIR), 1)
        for e in range(2):
            mine_t = (feature < DH) == (e == 0)
            mine = (lane < DH) == (e == 0)
            qtx[e, :PAIR] = jnp.where(mine_t, q_t, 0.0).astype(BF16)
            qtx[e, PAIR:] = jnp.where(feature == 0, 1.0, 0.0).astype(BF16)
            qm[e] = jnp.where(mine, q, 0.0).astype(BF16)
            gt8[e] = jnp.where(mine_t, grad_t * 0.125, 0.0).astype(BF16)
            gm[e] = jnp.where(mine, grad, 0.0).astype(BF16)

        arrived(0, g)

        def scores(i, carry):
            rows = rows_of(i)
            key = jnp.concatenate([wide[0, g, rows], bias[rows]], axis=1)
            new = []
            for e in range(2):
                peak, total = carry[e]
                s = dot(key, qtx[e])
                peak_now = jnp.maximum(peak, jnp.max(s, axis=0, keepdims=True))
                prob = jnp.exp2((s - peak_now) * EXPONENT)
                probs[e, rows] = prob
                maxima[e, i] = peak_now
                total = total * jnp.exp2((peak - peak_now) * EXPONENT)
                new.append((peak_now, total + jnp.sum(prob, axis=0, keepdims=True)))
            return tuple(new)

        none = (jnp.full((1, units), -1e38, F32), jnp.zeros((1, units), F32))
        stats = lax.fori_loop(0, chunks, scores, (none, none), unroll=UNROLL)
        inverse = [1.0 / stats[e][1] for e in range(2)]

        def factor(e, i):
            return jnp.exp2((maxima[e, i] - stats[e][0]) * EXPONENT) * inverse[e]

        att_t[...] = jnp.zeros_like(att_t)
        qg_t[...] = jnp.zeros_like(qg_t)

        def attend(i, _):
            rows = rows_of(i)
            value_t = wide[1, g, rows].T
            term = None
            for e in range(2):
                low = (probs[e, rows] * factor(e, i)).astype(BF16)
                half = slice(e * DH, (e + 1) * DH)
                att_t[half] += dot(value_t[half], low)
                part = dot(low, gm[e])
                term = part if term is None else term + part
            totals[1, g, rows] = term
            return 0

        arrived(1, g)
        lax.fori_loop(0, chunks, attend, 0, unroll=UNROLL)
        send_rims(1, g)

        attended = att_t[...].astype(BF16).astype(F32)
        att_ref[:, cols] = attended.T.astype(BF16)
        product = attended * grad_t * 0.125
        row_dot = [
            jnp.sum(product[e * DH:(e + 1) * DH], axis=0, keepdims=True) for e in range(2)
        ]

        def backward(i, _):
            rows = rows_of(i)
            value = wide[1, g, rows]
            key_t = wide[0, g, rows].T
            term = None
            for e in range(2):
                weight = probs[e, rows] * factor(e, i)
                score_grad = (weight * (dot(value, gt8[e]) - row_dot[e])).astype(BF16)
                half = slice(e * DH, (e + 1) * DH)
                qg_t[half] += dot(key_t[half], score_grad)
                part = dot(score_grad, qm[e])
                term = part if term is None else term + part
            totals[0, g, rows] = term
            return 0

        lax.fori_loop(0, chunks, backward, 0, unroll=UNROLL)
        send_rims(0, g)
        qg_ref[:, cols] = qg_t[...].T.astype(BF16)

        @pl.when(g > 0)
        def _():
            finish(g - 1)

        return 0

    lax.fori_loop(0, pairs, per_pair, 0)
    finish(pairs - 1)

    for g in range(pairs):
        for t in range(2):
            @pl.when(has_hi)
            def _():
                halo(t, g, 0).wait_send()
                rim(t, g, 0).wait_send()

            @pl.when(has_lo)
            def _():
                halo(t, g, 1).wait_send()
                rim(t, g, 1).wait_send()

            @pl.when(me == n - 2)
            def _():
                halo_far(t, g, 0).wait_send()

            @pl.when(me == 1)
            def _():
                halo_far(t, g, 1).wait_send()

            @pl.when(first)
            def _():
                rim_far(t, g, 0).wait_send()

            @pl.when(last)
            def _():
                rim_far(t, g, 1).wait_send()


def hand_on(*refs):
    srcs, dsts, sem = refs[:4], refs[4:8], refs[8]
    copies = []
    for a in range(4):
        part = srcs[a].shape[0] // PARTS
        for b in range(PARTS):
            rows = pl.ds(b * part, part)
            copies.append(pltpu.make_async_copy(srcs[a].at[rows], dsts[a].at[rows], sem.at[a, b]))
    for copy in copies:
        copy.start()
    for copy in copies:
        copy.wait()


def on_device(n, queries, keys, values, out_grad, band_start, band_len):
    units, width = queries.shape
    frames = keys.shape[0]
    pairs = width // PAIR
    span = frames + 2 * REACH
    dma = pltpu.SemaphoreType.DMA
    vmem = pl.BlockSpec(memory_space=pltpu.VMEM)
    smem = pl.BlockSpec(memory_space=pltpu.SMEM)
    anywhere = pl.BlockSpec(memory_space=pl.ANY)
    results = pl.pallas_call(
        functools.partial(kernel, n),
        out_shape=(
            jax.ShapeDtypeStruct((units, width), BF16),
            jax.ShapeDtypeStruct((units, width), BF16),
            jax.ShapeDtypeStruct((frames, width), BF16),
            jax.ShapeDtypeStruct((frames, width), BF16),
        ),
        in_specs=[smem, smem, vmem, vmem, anywhere, anywhere],
        out_specs=(vmem, vmem, vmem, vmem),
        scratch_shapes=[
            pltpu.VMEM((2, pairs, span, PAIR), BF16),
            pltpu.VMEM((span, PAIR), BF16),
            pltpu.VMEM((2, span, units), F32),
            pltpu.VMEM((2, span // CHUNK + 1, 1, units), F32),
            pltpu.VMEM((2, 2 * PAIR, units), BF16),
            pltpu.VMEM((2, units, PAIR), BF16),
            pltpu.VMEM((2, PAIR, units), BF16),
            pltpu.VMEM((2, units, PAIR), BF16),
            pltpu.VMEM((PAIR, units), F32),
            pltpu.VMEM((PAIR, units), F32),
            pltpu.VMEM((2, pairs, span, PAIR), F32),
            pltpu.VMEM((2, pairs, 2, REACH, PAIR), BF16),
            pltpu.VMEM((2, pairs, 2, REACH, PAIR), BF16),
            dma((2, pairs)),
        ] + [dma((2, pairs, 2))] * 8,
        compiler_params=pltpu.CompilerParams(
            collective_id=0, has_side_effects=True, vmem_limit_bytes=56 * 2**20
        ),
        name="banded",
    )(band_start, band_len, queries, out_grad, keys, values)
    return pl.pallas_call(
        hand_on,
        out_shape=tuple(jax.ShapeDtypeStruct(r.shape, r.dtype) for r in results),
        in_specs=[vmem] * 4,
        out_specs=(anywhere,) * 4,
        scratch_shapes=[dma((4, PARTS))],
        name="hand_on",
    )(*results)


def solution(mesh):
    rows = P(("groups", "tm"), None)
    return jax.shard_map(
        functools.partial(on_device, mesh.shape["tm"]),
        mesh=mesh,
        in_specs=(rows, rows, rows, rows, P("groups"), P("groups")),
        out_specs=(rows, rows, rows, rows),
        check_vma=False,
    )
```
